32 devices in a mesh: ew: 2 (over y), ns: 16 (over z, x, core).
Axes of the slice: x: 2, y: 2, z: 4, core: 2. Of those that a mesh axis runs over, the one named last changes fastest.
Arguments:
- couplings: bfloat16 [2, 16, 16, 128, 2048], P('ew', 'ns'), may hold values from -0.125 to 0.125
- inverses: bfloat16 [2, 16, 16, 128, 128], P('ew', 'ns'), as said below
- pattern: int32 [2, 16, 16, 16], P('ew', 'ns'), may hold values 0 or 1
- counts: int32 [2, 16], P('ew', 'ns'), may hold values from 1 to 16, as said below
- basis: bfloat16 [2, 16, 128, 512], P('ew', 'ns'), may hold values from -0.25 to 0.25
Outputs:
- south_front: float32 [2, 16, 768, 768], P('ew', 'ns')
- west_front: float32 [2, 16, 256, 256], P('ew', 'ns')
- coarse: float32 [2, 16, 128, 128], P('ew', 'ns')
The draws below stay inside these ranges and needn't reach their ends.
Inputs may be any that keep to these rules, and one draw needn't show every extreme that they name: `counts`: some subdomain has exactly 16 live block columns. `inverses`: each block is symmetric.
All inputs are finite; a program needn't handle non-finite values. No bound on the sum of `pattern` on one device may be relied on, other than what follows from the above.
Results may differ from the reference program's by a relative error of at most 0.0015.
Values may be sent and summed in bfloat16 or wider, within the bound.
A program may use at most 128 MiB of HBM per device.

```python
import jax
import jax.numpy as jnp
from jax import lax

B = 128
SN = 6
SE = 2
R = 128
K = 16
N_EW = 2
N_NS = 16


def draw_inverses(key, part):
    first, second = jax.random.split(jax.random.fold_in(key, 11))
    shape = (N_EW, N_NS, K, B, B)
    noise = jax.random.normal(first, shape, jnp.float32)
    symmetric = (noise + jnp.swapaxes(noise, -1, -2)) * (0.5 / jnp.sqrt(2.0 * B))
    diagonal = jax.random.uniform(second, shape[:-1], jnp.float32, 1.5, 3.0)
    identity = jnp.eye(B, dtype=jnp.float32)
    return (symmetric * (1.0 - identity) + diagonal[..., None] * identity).astype(jnp.bfloat16)


def draw_counts(key, part):
    first, second = jax.random.split(jax.random.fold_in(key, 23))
    base = jax.random.randint(first, (N_EW, N_NS), 1, K + 1)
    picked = jax.random.randint(second, (), 0, N_EW * N_NS)
    places = jnp.arange(N_EW * N_NS, dtype=jnp.int32).reshape(N_EW, N_NS)
    return jnp.where(places == picked, K, base).astype(jnp.int32)


def plant(drawn, stream_key, smallest, high):
    longest = drawn.shape.index(max(drawn.shape))
    spots = []
    for shift in (0, 1):
        where = [jax.random.randint(jax.random.fold_in(stream_key, axis), (), 0, length) for axis, length in enumerate(drawn.shape)]
        where[longest] = (where[longest] + shift) % drawn.shape[longest]
        spots.append(tuple(where))
    return drawn.at[spots[0]].set(smallest).at[spots[1]].set(high)


def level_of(stream_key, shape, pieces, smallest, largest):
    loudness = 1.0
    for dim, shards_of in pieces:
        steps = jax.random.uniform(jax.random.fold_in(jax.random.fold_in(stream_key, 6), dim), (shards_of,), jnp.float32, smallest / len(pieces), largest / len(pieces))
        loudness = loudness * jnp.repeat(jnp.exp(steps), shape[dim] // shards_of).reshape((-1,) + (1,) * (len(shape) - 1 - dim))
    return loudness


def normal_values(own_key, shape, deviation, reach, shards=(), kind=jnp.bfloat16):
    array = jax.random.normal(own_key, shape, jnp.float32) * deviation
    if len(shards) > 0:
        array = level_of(own_key, shape, shards, -0.22, 0.18) * array
    return jnp.clip(array, min=-reach, max=reach).astype(kind)


def setup_inputs(seed: int = 0) -> dict:
    key_list = jax.random.split(jax.random.key(seed), 6)
    return {
        "couplings": normal_values(key_list[0], (N_EW, N_NS, K, B, (2 * SN + 2 * SE) * B), (K * B) ** -0.5, 0.125, ((0, 2), (1, 16))),
        "inverses": draw_inverses(jax.random.fold_in(key_list[5], 71), 0),
        "pattern": plant((jax.random.randint(key_list[2], (N_EW, N_NS, K, 2 * SN + 2 * SE), 0, 4) < 3).astype(jnp.int32), jax.random.fold_in(key_list[2], 1), 0, 1),
        "counts": draw_counts(jax.random.fold_in(key_list[5], 71), 0),
        "basis": normal_values(key_list[4], (N_EW, N_NS, R, N_EW * SE * B), (N_EW * SE * B) ** -0.5, 0.25, ((0, 2), (1, 16))),
    }


def edge_update(slab, inverse):
    solved = jnp.einsum('kab,kbc->kac', inverse.astype(jnp.float32), slab.astype(jnp.float32)).astype(jnp.bfloat16)
    return -jnp.einsum('kbi,kbj->ij', slab.astype(jnp.float32), solved.astype(jnp.float32))


def device_updates(items):
    coupling, inverse, touched, count = items
    columns = jnp.repeat(touched, B, axis=1)
    live = (jnp.arange(K, dtype=jnp.int32) < count).astype(jnp.int32)[:, None]
    keep = (columns * live).astype(jnp.bfloat16)
    masked = coupling * keep[:, None, :]
    north_start = SN * B
    west_start = 2 * SN * B
    east_start = west_start + SE * B
    south_part = edge_update(masked[:, :, 0:north_start], inverse)
    north_part = edge_update(masked[:, :, north_start:west_start], inverse)
    west_part = edge_update(masked[:, :, west_start:east_start], inverse)
    east_part = edge_update(masked[:, :, east_start:east_start + SE * B], inverse)
    return south_part, north_part, west_part, east_part


def reference(couplings, inverses, pattern, counts, basis):
    width = (2 * SN + 2 * SE) * B
    flat = (couplings.reshape(N_EW * N_NS, K, B, width), inverses.reshape(N_EW * N_NS, K, B, B),
            pattern.reshape(N_EW * N_NS, K, 2 * SN + 2 * SE), counts.reshape(N_EW * N_NS))
    south_part, north_part, west_part, east_part = lax.map(device_updates, flat)
    south_part = south_part.reshape(N_EW, N_NS, SN * B, SN * B)
    north_part = north_part.reshape(N_EW, N_NS, SN * B, SN * B)
    west_part = west_part.reshape(N_EW, N_NS, SE * B, SE * B)
    east_part = east_part.reshape(N_EW, N_NS, SE * B, SE * B)
    from_south = jnp.concatenate([jnp.zeros_like(north_part[:, :1]), north_part[:, :-1]], axis=1)
    south_front = south_part + from_south
    from_west = jnp.concatenate([jnp.zeros_like(east_part[:1]), east_part[:-1]], axis=0)
    west_front = west_part + from_west
    front_half = west_front.astype(jnp.bfloat16)
    blocks = basis.reshape(N_EW, N_NS, R, N_EW, SE * B).astype(jnp.float32)
    projected = jnp.einsum('enrjk,jnkl->enrjl', blocks, front_half.astype(jnp.float32)).astype(jnp.bfloat16)
    coarse = jnp.einsum('enrjl,ensjl->enrs', projected.astype(jnp.float32), blocks)
    return south_front, west_front, coarse
```

```python
import functools

import jax
import jax.numpy as jnp
from jax import lax
from jax.experimental import pallas as pl
from jax.experimental.pallas import tpu as pltpu
from jax.sharding import PartitionSpec as P

B = 128
SN = 6
SE = 2
T = 256
MESH = pl.DeviceIdType.MESH
TOP = 32767.0


def dot_tn(a, b):
    return lax.dot_general(a, b, (((0,), (0,)), ((), ())), preferred_element_type=jnp.float32)


def dot_nn(a, b):
    return lax.dot_general(a, b, (((1,), (0,)), ((), ())), preferred_element_type=jnp.float32)


def dot_nt(a, b):
    return lax.dot_general(a, b, (((1,), (1,)), ((), ())), preferred_element_type=jnp.float32)


def encode(block):
    top = jnp.maximum(jnp.max(jnp.abs(block), axis=0, keepdims=True), 2e-34)
    code = jnp.round(block * (TOP / top)).astype(jnp.int32).astype(jnp.int16)
    return code, top * (1.0 / TOP)


def decode(code, scale):
    return code.astype(jnp.int32).astype(jnp.float32) * scale


def kernel(
    n_ew, n_ns, depth,
    coup, inv, pat, cnt, bas,
    south, west, coarse,
    cm, am, qm, keep, solved,
    off_out, dia_out, sca_out, off_in, dia_in, sca_in,
    east_out, east_in, fronts,
    load_sem, send_sem, recv_sem, esend, erecv, gsend, grecv,
):
    e = lax.axis_index("ew")
    n = lax.axis_index("ns")
    has_next = n < n_ns - 1
    has_prev = n > 0
    north0 = SN * B
    west0 = 2 * SN * B
    east0 = west0 + SE * B
    stripes = SN * B // T

    barrier = pltpu.get_barrier_semaphore()

    @pl.when(has_prev)
    def _():
        pl.semaphore_signal(barrier, inc=1, device_id=(e, n - 1), device_id_type=MESH)

    @pl.when(has_next)
    def _():
        pl.semaphore_signal(barrier, inc=1, device_id=(e, n + 1), device_id_type=MESH)

    for d in range(1, n_ew):
        pl.semaphore_signal(
            barrier, inc=1, device_id=(lax.rem(e + d, n_ew), n), device_id_type=MESH
        )

    copies = {}

    def load(name, src, dst):
        copies[name] = pltpu.make_async_copy(src, dst, load_sem.at[len(copies)])
        copies[name].start()

    load("inv", inv, am)
    for name, start, width in (
        ("north", north0, SN * B),
        ("east", east0, SE * B),
        ("west", west0, SE * B),
        ("south", 0, SN * B),
    ):
        load(name, coup.at[:, pl.ds(start, width)], cm.at[:, pl.ds(start, width)])
    load("bas", bas, qm)

    blocks = pat.shape[1]
    lane = lax.broadcasted_iota(jnp.int32, (blocks, blocks * B), 1)
    row = lax.broadcasted_iota(jnp.int32, (blocks, blocks * B), 0)
    spread = jnp.where((lane >= row * B) & (lane < row * B + B), 1.0, 0.0).astype(jnp.bfloat16)
    live = lax.broadcasted_iota(jnp.int32, pat.shape, 0) < cnt[0, 0]
    touched = jnp.where(live, pat[...], 0).astype(jnp.float32).astype(jnp.bfloat16)
    keep[...] = dot_nn(touched, spread)

    @pl.when(n == 0)
    def _():
        off_in[...] = jnp.zeros_like(off_in)
        dia_in[...] = jnp.zeros_like(dia_in)
        sca_in[...] = jnp.zeros_like(sca_in)

    @pl.when(e == 0)
    def _():
        east_in[...] = jnp.zeros_like(east_in)

    def mask(start, width):
        for k in range(depth):
            rows = slice(k * B, k * B + B)
            cols = slice(start, start + width)
            cm[rows, cols] = cm[rows, cols] * keep[k : k + 1, cols].astype(jnp.bfloat16)

    def solve(start):
        for k in range(depth):
            rows = slice(k * B, k * B + B)
            solved[rows, :] = dot_nn(am[rows, :], cm[rows, start : start + T]).astype(jnp.bfloat16)

    def tile(start):
        return -dot_tn(cm[:, start : start + T], solved[...])

    def to_next(j):
        device = (e, n + 1)
        out = []
        sem = 3 * j
        if j < stripes - 1:
            first = j * (2 * stripes - 1 - j) // 2
            span = pl.ds(first, stripes - 1 - j)
            out.append((off_out.at[span], off_in.at[span], sem))
        out.append((dia_out.at[j], dia_in.at[j], sem + 1))
        out.append((sca_out.at[j], sca_in.at[j], sem + 2))
        return [
            pltpu.make_async_remote_copy(
                src_ref=s, dst_ref=d, send_sem=send_sem.at[m], recv_sem=recv_sem.at[m],
                device_id=device, device_id_type=MESH,
            )
            for s, d, m in out
        ]

    def north_stripe(j):
        solve(north0 + j * T)
        first = j * (2 * stripes - 1 - j) // 2
        for i in range(j + 1, stripes):
            code, scale = encode(tile(north0 + i * T))
            off_out[first + i - j - 1] = code
            sca_out[j, i - j - 1 : i - j, :] = scale
        t = tile(north0 + j * T)
        for b, (r, c) in enumerate(((0, 0), (1, 0), (1, 1))):
            code, scale = encode(t[r * B : r * B + B, c * B : c * B + B])
            dia_out[j, b * B : b * B + B, :] = code
            sca_out[j, 4 + b : 5 + b, 0:B] = scale
        if j == 0:
            peers = n_ew - 1 + has_prev.astype(jnp.int32) + has_next.astype(jnp.int32)
            pl.semaphore_wait(barrier, peers)

        @pl.when(has_next)
        def _():
            for c in to_next(j):
                c.start()

    sca_out[...] = jnp.zeros_like(sca_out)
    copies["inv"].wait()
    copies["north"].wait()
    mask(north0, SN * B)
    north_stripe(0)

    copies["east"].wait()
    mask(east0, SE * B)
    solve(east0)
    east_out[...] = tile(east0)
    east_copy = pltpu.make_async_remote_copy(
        src_ref=east_out, dst_ref=east_in, send_sem=esend, recv_sem=erecv,
        device_id=(e + 1, n), device_id_type=MESH,
    )

    @pl.when(e < n_ew - 1)
    def _():
        east_copy.start()

    for j in range(1, stripes):
        north_stripe(j)

    copies["west"].wait()
    mask(west0, SE * B)
    solve(west0)
    west[...] = tile(west0)

    copies["south"].wait()
    mask(0, SN * B)
    for j in range(stripes):
        solve(j * T)
        for i in range(j, stripes):
            south[i * T : i * T + T, j * T : j * T + T] = tile(i * T)

    @pl.when(e > 0)
    def _():
        east_copy.wait_recv()

    front = west[...] + east_in[...]
    west[...] = front
    fronts[e] = front.astype(jnp.bfloat16)

    def gather(d):
        return pltpu.make_async_remote_copy(
            src_ref=fronts.at[e], dst_ref=fronts.at[e], send_sem=gsend.at[d - 1],
            recv_sem=grecv.at[d - 1], device_id=(lax.rem(e + d, n_ew), n), device_id_type=MESH,
        )

    for d in range(1, n_ew):
        gather(d).start()

    def finish(j):
        @pl.when(has_prev)
        def _():
            for c in to_next(j):
                c.wait_recv()

        first = j * (2 * stripes - 1 - j) // 2
        cols = slice(j * T, j * T + T)
        for i in range(j + 1, stripes):
            rows = slice(i * T, i * T + T)
            scale = sca_in[j, i - j - 1 : i - j, :]
            total = south[rows, cols] + decode(off_in[first + i - j - 1], scale)
            south[rows, cols] = total
            south[cols, rows] = total.T
        o = j * T
        parts = [
            decode(dia_in[j, b * B : b * B + B, :], sca_in[j, 4 + b : 5 + b, 0:B]) for b in range(3)
        ]
        south[o : o + B, o : o + B] += parts[0]
        south[o + B : o + T, o + B : o + T] += parts[2]
        low = south[o + B : o + T, o : o + B] + parts[1]
        south[o + B : o + T, o : o + B] = low
        south[o : o + B, o + B : o + T] = low.T

    for j in range(stripes - 1):
        finish(j)

    copies["bas"].wait()
    total = jnp.zeros(coarse.shape, jnp.float32)
    for d in range(n_ew):
        if d > 0:
            gather(d).wait_recv()
        j = lax.rem(e + n_ew - d, n_ew)
        q = qm[:, pl.ds(pl.multiple_of(j * SE * B, SE * B), SE * B)]
        projected = dot_nn(q, fronts[j]).astype(jnp.bfloat16)
        total = total + dot_nt(projected, q)
    coarse[...] = total

    finish(stripes - 1)

    for d in range(1, n_ew):
        gather(d).wait_send()

    @pl.when(e < n_ew - 1)
    def _():
        east_copy.wait_send()

    @pl.when(has_next)
    def _():
        for j in range(stripes):
            for c in to_next(j):
                c.wait_send()


def shards(n_ew, n_ns, couplings, inverses, pattern, counts, basis):
    depth = couplings.shape[2]
    width = couplings.shape[4]
    coup = couplings.reshape(depth * B, width)
    inv = inverses.reshape(depth * B, B)
    pat = pattern[0, 0]
    bas = basis[0, 0]
    stripes = SN * B // T
    offs = stripes * (stripes - 1) // 2
    east = SE * B
    f32, bf16, i16 = jnp.float32, jnp.bfloat16, jnp.int16
    vmem = pl.BlockSpec(memory_space=pltpu.VMEM)
    anyspace = pl.BlockSpec(memory_space=pltpu.HBM)
    south, west, coarse = pl.pallas_call(
        functools.partial(kernel, n_ew, n_ns, depth),
        out_shape=(
            jax.ShapeDtypeStruct((SN * B, SN * B), f32),
            jax.ShapeDtypeStruct((east, east), f32),
            jax.ShapeDtypeStruct((bas.shape[0], bas.shape[0]), f32),
        ),
        in_specs=[anyspace, anyspace, vmem, pl.BlockSpec(memory_space=pltpu.SMEM), anyspace],
        out_specs=(vmem, vmem, vmem),
        scratch_shapes=[
            pltpu.VMEM((depth * B, width), bf16),
            pltpu.VMEM((depth * B, B), bf16),
            pltpu.VMEM(bas.shape, bf16),
            pltpu.VMEM((depth, width), f32),
            pltpu.VMEM((depth * B, T), bf16),
            pltpu.VMEM((offs, T, T), i16),
            pltpu.VMEM((stripes, 3 * B, B), i16),
            pltpu.VMEM((stripes, 8, T), f32),
            pltpu.VMEM((offs, T, T), i16),
            pltpu.VMEM((stripes, 3 * B, B), i16),
            pltpu.VMEM((stripes, 8, T), f32),
            pltpu.VMEM((east, east), f32),
            pltpu.VMEM((east, east), f32),
            pltpu.VMEM((n_ew, east, east), bf16),
            pltpu.SemaphoreType.DMA((6,)),
            pltpu.SemaphoreType.DMA((3 * stripes,)),
            pltpu.SemaphoreType.DMA((3 * stripes,)),
            pltpu.SemaphoreType.DMA,
            pltpu.SemaphoreType.DMA,
            pltpu.SemaphoreType.DMA((max(n_ew - 1, 1),)),
            pltpu.SemaphoreType.DMA((max(n_ew - 1, 1),)),
        ],
        compiler_params=pltpu.CompilerParams(
            collective_id=0, has_side_effects=True, vmem_limit_bytes=60 * 2**20
        ),
        cost_estimate=pl.CostEstimate(
            flops=5 * 10**9, bytes_accessed=12 * 10**6, transcendentals=0
        ),
        name="fronts",
    )(coup, inv, pat, counts, bas)
    return (south[None, None], west[None, None], coarse[None, None])


def solution(mesh):
    sizes = (mesh.shape["ew"], mesh.shape["ns"])
    return jax.shard_map(
        functools.partial(shards, *sizes),
        mesh=mesh,
        in_specs=(
            P("ew", "ns", None, None, None),
            P("ew", "ns", None, None, None),
            P("ew", "ns", None, None),
            P("ew", "ns"),
            P("ew", "ns", None, None),
        ),
        out_specs=(P("ew", "ns", None, None), P("ew", "ns", None, None), P("ew", "ns", None, None)),
        check_vma=False,
    )
```

```python
import functools

import jax
import jax.numpy as jnp
from jax import lax
from jax.experimental import pallas as pl
from jax.experimental.pallas import tpu as pltpu
from jax.sharding import PartitionSpec as P

B = 128
SN = 6
SE = 2
T = 256
XPOSE, WIDE, REMOTE = 'xlu', 1, 1
MESH = pl.DeviceIdType.MESH
TOP = 32767.0


def dot_tn(a, b):
    return lax.dot_general(a, b, (((0,), (0,)), ((), ())), preferred_element_type=jnp.float32)


def dot_nn(a, b):
    return lax.dot_general(a, b, (((1,), (0,)), ((), ())), preferred_element_type=jnp.float32)


def dot_nt(a, b):
    return lax.dot_general(a, b, (((1,), (1,)), ((), ())), preferred_element_type=jnp.float32)


def encode(block):
    top = jnp.maximum(jnp.max(jnp.abs(block), axis=0, keepdims=True), 2e-34)
    code = jnp.round(block * (TOP / top)).astype(jnp.int32).astype(jnp.int16)
    return code, top * (1.0 / TOP)


def decode(code, scale):
    return code.astype(jnp.int32).astype(jnp.float32) * scale


def kernel(
    n_ew, n_ns, depth,
    coup, inv, pat, cnt, bas,
    south, west, coarse,
    cm, ct, am, qm, keep, solved,
    off_out, dia_out, sca_out, off_in, dia_in, sca_in,
    east_out, east_in, fronts,
    load_sem, send_sem, recv_sem, esend, erecv, gsend, grecv,
):
    e = lax.axis_index("ew")
    n = lax.axis_index("ns")
    has_next = n < n_ns - 1
    has_prev = n > 0
    north0 = SN * B
    west0 = 2 * SN * B
    east0 = west0 + SE * B
    stripes = SN * B // T

    barrier = pltpu.get_barrier_semaphore()

    @pl.when(has_prev)
    def _():
        pl.semaphore_signal(barrier, inc=1, device_id=(e, n - 1), device_id_type=MESH)

    @pl.when(has_next)
    def _():
        pl.semaphore_signal(barrier, inc=1, device_id=(e, n + 1), device_id_type=MESH)

    for d in range(1, n_ew):
        pl.semaphore_signal(
            barrier, inc=1, device_id=(lax.rem(e + d, n_ew), n), device_id_type=MESH
        )

    copies = {}

    def load(name, src, dst):
        copies[name] = pltpu.make_async_copy(src, dst, load_sem.at[len(copies)])
        copies[name].start()

    pairs = depth // 2
    am[:, 0:B, B:T] = jnp.zeros((pairs, B, B), am.dtype)
    am[:, B:T, 0:B] = jnp.zeros((pairs, B, B), am.dtype)
    for p in range(2):
        half = pl.ds(p * B, B)
        load(("inv", p), inv.at[:, p], am.at[:, half, half])
    parts = 4
    span = depth * B // parts
    for p in range(parts):
        rows, cols = pl.ds(p * span, span), pl.ds(north0, SN * B)
        load(("north", p), coup.at[rows, cols], cm.at[rows, cols])
    for name, start, width in (
        ("east", east0, SE * B),
        ("west", west0, SE * B),
        ("south", 0, SN * B),
    ):
        load(name, coup.at[:, pl.ds(start, width)], cm.at[:, pl.ds(start, width)])
    load("bas", bas, qm)

    blocks = pat.shape[1]
    lane = lax.broadcasted_iota(jnp.int32, (blocks, blocks * B), 1)
    row = lax.broadcasted_iota(jnp.int32, (blocks, blocks * B), 0)
    spread = jnp.where((lane >= row * B) & (lane < row * B + B), 1.0, 0.0).astype(jnp.bfloat16)
    live = lax.broadcasted_iota(jnp.int32, pat.shape, 0) < cnt[0, 0]
    touched = jnp.where(live, pat[...], 0).astype(jnp.float32).astype(jnp.bfloat16)
    keep[...] = dot_nn(touched, spread)

    @pl.when(n == 0)
    def _():
        sca_in[...] = jnp.zeros_like(sca_in)

    def turn(block):
        if XPOSE == 'xlu':
            return block.T
        return dot_nt(eye, block).astype(jnp.bfloat16)

    eye = (
        lax.broadcasted_iota(jnp.int32, (T, T), 0) == lax.broadcasted_iota(jnp.int32, (T, T), 1)
    ).astype(jnp.float32).astype(jnp.bfloat16)

    def mask(start, width, first=0, last=depth):
        for k in range(first, last, 2):
            rows = slice(k * B, k * B + T)
            for c in range(start, start + width, T):
                cols = slice(c, c + T)
                wide = jnp.concatenate(
                    [jnp.broadcast_to(keep[k + p : k + p + 1, cols], (B, T)) for p in range(2)]
                ).astype(jnp.bfloat16)
                masked = cm[rows, cols] * wide
                cm[rows, cols] = masked
                ct[cols, rows] = turn(masked)

    def solve(start):
        for k in range(pairs):
            rows = slice(k * T, k * T + T)
            solved[rows, :] = dot_nn(am[k], cm[rows, start : start + T]).astype(jnp.bfloat16)

    def tile(start):
        return -dot_nn(ct[start : start + T, :], solved[...])

    def tiles(start, end):
        if WIDE:
            whole = -dot_nn(ct[start:end, :], solved[...])
            return [whole[o : o + T] for o in range(0, end - start, T)]
        return [tile(o) for o in range(start, end, T)]

    def to_next(j):
        device = (e, n + 1)
        if not REMOTE:
            return []
        out = []
        sem = 3 * j
        if j < stripes - 1:
            first = j * (2 * stripes - 1 - j) // 2
            span = pl.ds(first, stripes - 1 - j)
            out.append((off_out.at[span], off_in.at[span], sem))
        out.append((dia_out.at[j], dia_in.at[j], sem + 1))
        out.append((sca_out.at[j], sca_in.at[j], sem + 2))
        return [
            pltpu.make_async_remote_copy(
                src_ref=s, dst_ref=d, send_sem=send_sem.at[m], recv_sem=recv_sem.at[m],
                device_id=device, device_id_type=MESH,
            )
            for s, d, m in out
        ]

    def north_stripe(j):
        solve(north0 + j * T)
        first = j * (2 * stripes - 1 - j) // 2
        results = tiles(north0 + j * T, north0 + SN * B)
        for i in range(j + 1, stripes):
            code, scale = encode(results[i - j])
            off_out[first + i - j - 1] = code
            sca_out[j, i - j - 1 : i - j, :] = scale
        t = results[0]
        for b, (r, c) in enumerate(((0, 0), (1, 0), (1, 1))):
            code, scale = encode(t[r * B : r * B + B, c * B : c * B + B])
            dia_out[j, b * B : b * B + B, :] = code
            sca_out[j, 4 + b : 5 + b, 0:B] = scale
        if j == 0:
            peers = n_ew - 1 + has_prev.astype(jnp.int32) + has_next.astype(jnp.int32)
            pl.semaphore_wait(barrier, peers)

        @pl.when(has_next)
        def _():
            for c in to_next(j):
                c.start()

    sca_out[...] = jnp.zeros_like(sca_out)
    for p in range(2):
        copies["inv", p].wait()
    for p in range(parts):
        copies["north", p].wait()
        mask(north0, SN * B, p * depth // parts, (p + 1) * depth // parts)
    north_stripe(0)

    copies["east"].wait()
    mask(east0, SE * B)
    solve(east0)
    east_out[...] = tile(east0)
    east_copy = pltpu.make_async_remote_copy(
        src_ref=east_out, dst_ref=east_in, send_sem=esend, recv_sem=erecv,
        device_id=(e + 1, n), device_id_type=MESH,
    )

    @pl.when(e < n_ew - 1)
    def _():
        east_copy.start()

    for j in range(1, stripes):
        north_stripe(j)

    copies["west"].wait()
    mask(west0, SE * B)
    solve(west0)
    west[...] = tile(west0)

    copies["south"].wait()
    mask(0, SN * B)
    for j in range(stripes):
        solve(j * T)
        for i, result in enumerate(tiles(j * T, SN * B), j):
            south[i * T : i * T + T, j * T : j * T + T] = result

    @pl.when(e > 0)
    def _():
        east_copy.wait_recv()

    front = west[...] + jnp.where(e > 0, east_in[...], 0.0)
    west[...] = front
    fronts[e] = front.astype(jnp.bfloat16)

    def gather(d):
        return pltpu.make_async_remote_copy(
            src_ref=fronts.at[e], dst_ref=fronts.at[e], send_sem=gsend.at[d - 1],
            recv_sem=grecv.at[d - 1], device_id=(lax.rem(e + d, n_ew), n), device_id_type=MESH,
        )

    for d in range(1, n_ew):
        gather(d).start()

    def finish(j):
        @pl.when(has_prev)
        def _():
            for c in to_next(j):
                c.wait_recv()

        first = j * (2 * stripes - 1 - j) // 2
        cols = slice(j * T, j * T + T)
        for i in range(j + 1, stripes):
            rows = slice(i * T, i * T + T)
            scale = sca_in[j, i - j - 1 : i - j, :]
            total = south[rows, cols] + decode(off_in[first + i - j - 1], scale)
            south[rows, cols] = total
            south[cols, rows] = total.T
        o = j * T
        parts = [
            decode(dia_in[j, b * B : b * B + B, :], sca_in[j, 4 + b : 5 + b, 0:B]) for b in range(3)
        ]
        south[o : o + B, o : o + B] += parts[0]
        south[o + B : o + T, o + B : o + T] += parts[2]
        low = south[o + B : o + T, o : o + B] + parts[1]
        south[o + B : o + T, o : o + B] = low
        south[o : o + B, o + B : o + T] = low.T

    for j in range(stripes - 1):
        finish(j)

    copies["bas"].wait()
    total = jnp.zeros(coarse.shape, jnp.float32)
    for d in range(n_ew):
        if d > 0:
            gather(d).wait_recv()
        j = lax.rem(e + n_ew - d, n_ew)
        q = qm[:, pl.ds(pl.multiple_of(j * SE * B, SE * B), SE * B)]
        projected = dot_nn(q, fronts[j]).astype(jnp.bfloat16)
        total = total + dot_nt(projected, q)
    coarse[...] = total

    finish(stripes - 1)

    for d in range(1, n_ew):
        gather(d).wait_send()

    @pl.when(e < n_ew - 1)
    def _():
        east_copy.wait_send()

    @pl.when(has_next)
    def _():
        for j in range(stripes):
            for c in to_next(j):
                c.wait_send()


def write_out(south_in, west_in, coarse_in, south, west, coarse, sems):
    copies = [
        pltpu.make_async_copy(a, b, sems.at[m])
        for m, (a, b) in enumerate(((south_in, south), (west_in, west), (coarse_in, coarse)))
    ]
    for c in copies:
        c.start()
    for c in copies:
        c.wait()


def shards(n_ew, n_ns, couplings, inverses, pattern, counts, basis):
    depth = couplings.shape[2]
    width = couplings.shape[4]
    coup = couplings.reshape(depth * B, width)
    inv = inverses.reshape(depth // 2, 2, B, B)
    pat = pattern[0, 0]
    bas = basis[0, 0]
    stripes = SN * B // T
    offs = stripes * (stripes - 1) // 2
    east = SE * B
    f32, bf16, i16 = jnp.float32, jnp.bfloat16, jnp.int16
    vmem = pl.BlockSpec(memory_space=pltpu.VMEM)
    anyspace = pl.BlockSpec(memory_space=pltpu.HBM)
    south, west, coarse = pl.pallas_call(
        functools.partial(kernel, n_ew, n_ns, depth),
        out_shape=(
            jax.ShapeDtypeStruct((SN * B, SN * B), f32),
            jax.ShapeDtypeStruct((east, east), f32),
            jax.ShapeDtypeStruct((bas.shape[0], bas.shape[0]), f32),
        ),
        in_specs=[anyspace, anyspace, vmem, pl.BlockSpec(memory_space=pltpu.SMEM), anyspace],
        out_specs=(vmem, vmem, vmem),
        scratch_shapes=[
            pltpu.VMEM((depth * B, width), bf16),
            pltpu.VMEM((width, depth * B), bf16),
            pltpu.VMEM((depth // 2, T, T), bf16),
            pltpu.VMEM(bas.shape, bf16),
            pltpu.VMEM((depth, width), f32),
            pltpu.VMEM((depth * B, T), bf16),
            pltpu.VMEM((offs, T, T), i16),
            pltpu.VMEM((stripes, 3 * B, B), i16),
            pltpu.VMEM((stripes, 8, T), f32),
            pltpu.VMEM((offs, T, T), i16),
            pltpu.VMEM((stripes, 3 * B, B), i16),
            pltpu.VMEM((stripes, 8, T), f32),
            pltpu.VMEM((east, east), f32),
            pltpu.VMEM((east, east), f32),
            pltpu.VMEM((n_ew, east, east), bf16),
            pltpu.SemaphoreType.DMA((10,)),
            pltpu.SemaphoreType.DMA((3 * stripes,)),
            pltpu.SemaphoreType.DMA((3 * stripes,)),
            pltpu.SemaphoreType.DMA,
            pltpu.SemaphoreType.DMA,
            pltpu.SemaphoreType.DMA((max(n_ew - 1, 1),)),
            pltpu.SemaphoreType.DMA((max(n_ew - 1, 1),)),
        ],
        compiler_params=pltpu.CompilerParams(
            collective_id=0, has_side_effects=True, vmem_limit_bytes=50 * 2**20
        ),
        cost_estimate=pl.CostEstimate(
            flops=5 * 10**9, bytes_accessed=12 * 10**6, transcendentals=0
        ),
        name="fronts",
    )(coup, inv, pat, counts, bas)
    whole = (south, west, coarse)
    south, west, coarse = pl.pallas_call(
        write_out,
        out_shape=[jax.ShapeDtypeStruct(x.shape, x.dtype) for x in whole],
        in_specs=[pl.BlockSpec(memory_space=pltpu.VMEM)] * 3,
        compiler_params=pltpu.CompilerParams(vmem_limit_bytes=4 * 2**20),
        out_specs=[pl.BlockSpec(memory_space=pltpu.HBM)] * 3,
        scratch_shapes=[pltpu.SemaphoreType.DMA((3,))],
        name="write_out",
    )(*whole)
    return (south[None, None], west[None, None], coarse[None, None])


def solution(mesh):
    sizes = (mesh.shape["ew"], mesh.shape["ns"])
    return jax.shard_map(
        functools.partial(shards, *sizes),
        mesh=mesh,
        in_specs=(
            P("ew", "ns", None, None, None),
            P("ew", "ns", None, None, None),
            P("ew", "ns", None, None),
            P("ew", "ns"),
            P("ew", "ns", None, None),
        ),
        out_specs=(P("ew", "ns", None, None), P("ew", "ns", None, None), P("ew", "ns", None, None)),
        check_vma=False,
    )
```
